32 devices in a mesh: lev: 8 (over z, x), mem: 4 (over y, core).
Axes of the slice: x: 2, y: 2, z: 4, core: 2. Of those that a mesh axis runs over, the one named last changes fastest.
Arguments:
- control: bfloat16 [8, 5, 128, 1024], P('mem', None, 'lev'), may hold values from -6 to 6
- static_control_vector: bfloat16 [5, 128, 1024], P(None, None, 'lev'), may hold values from -6 to 6
- perturb: bfloat16 [8, 5, 128, 1024], P('mem', None, None, 'lev'), may hold values from -6 to 6
- tiles: bfloat16 [4, 64, 64], replicated, may hold values from -0.375 to 0.375
- block_offset: int32 [16, 4], replicated, may hold values from -8 to 8
- vert: bfloat16 [5, 128, 128], replicated, may hold values from -0.5 to 0.5
- static_vertical_root: bfloat16 [5, 128, 128], replicated, may hold values from -0.5 to 0.5
- obs_index: int32 [32768], P(('lev', 'mem')), may hold values from 0 to 20479
- obs_value: float32 [32768], P(('lev', 'mem')), may hold values from -6 to 6
- obs_sigma: float32 [32768], P(('lev', 'mem')), may hold values from 0.3 to 1
- huber_mask: int32 [32768], P(('lev', 'mem')), may hold values 0 or 1
Outputs:
- control_out: bfloat16 [8, 5, 128, 1024], P('mem', None, 'lev')
- static_out: bfloat16 [5, 128, 1024], P(None, None, 'lev')
The draws below stay inside these ranges and needn't reach their ends.
Inputs may be any that keep to these rules, and one draw needn't show every extreme that they name: `obs_index`: indices count in the block held by the observation's own device: 5 variables, 128 / 4 levels, 128 columns, in that order. `block_offset`: source blocks wrap around the window.
All inputs are finite; a program needn't handle non-finite values. No bound on the sum of `huber_mask` on one device may be relied on, other than what follows from the above.
Results may differ from the reference program's by a relative error of at most 0.0057.
Values may be sent and summed in bfloat16 or wider, within the bound.
A program may use at most 64 MiB of HBM per device.

```python
import math
import jax
import jax.numpy as jnp
from jax import lax

V = 5
LEVELS = 128
BLOCK = 64
KNB = 4
COL_DEV = 128
ITERS = 2
M = 8
COLS = 1024
NBLK = 16
OBS = 32768
N_LEV = 8
N_MEM = 4


def place_ends(values, key, low, top_value):
    dims = values.shape
    place = [jax.random.randint(jax.random.fold_in(key, axis), (), 0, dims[axis]) for axis in range(len(dims))]
    values = values.at[tuple(place)].set(low)
    longest = dims.index(max(dims))
    place[longest] = (place[longest] + 1) % dims[longest]
    return values.at[tuple(place)].set(top_value)


def shard_levels(stream_key, dims, split, smallest, top_value):
    level = 1.0
    for dim, shards_of in split:
        heights = jax.random.uniform(jax.random.fold_in(jax.random.fold_in(stream_key, 6), dim), (shards_of,), jnp.float32, smallest / len(split), top_value / len(split))
        level = level * jnp.repeat(jnp.exp(heights), dims[dim] // shards_of).reshape((-1,) + (1,) * (len(dims) - 1 - dim))
    return level


def noise(stream_key, shape, spread, limit, pieces=(), kind=jnp.bfloat16):
    entries = spread * jax.random.normal(stream_key, shape, jnp.float32)
    if pieces:
        entries = entries * shard_levels(stream_key, shape, pieces, -0.22, 0.18)
    return jnp.clip(entries, -limit, limit).astype(kind)


def setup_inputs(seed: int = 0) -> dict:
    key_list = jax.random.split(jax.random.key(seed), 12)
    control = noise(key_list[0], (M, V, LEVELS, COLS), 1.0, 6.0, ((0, 4), (2, 8)))
    static_control_vector = noise(key_list[1], (V, LEVELS, COLS), 1.0, 6.0, ((2, 8),))
    perturb = noise(key_list[2], (M, V, LEVELS, COLS), 1.0, 6.0, ((0, 4), (3, 8)))
    tiles = noise(key_list[3], (KNB, BLOCK, BLOCK), (BLOCK * KNB) ** -0.5, 0.375)
    block_offset = place_ends(jax.random.randint(key_list[4], (NBLK, KNB), -8, 9), jax.random.fold_in(key_list[4], 1), -8, 8).astype(jnp.int32)
    vert = noise(key_list[5], (V, LEVELS, LEVELS), LEVELS ** -0.5, 0.5)
    static_vertical_root = noise(key_list[6], (V, LEVELS, LEVELS), LEVELS ** -0.5, 0.5)
    obs_index = place_ends(jax.random.randint(key_list[7], (OBS,), 0, V * (LEVELS // N_MEM) * COL_DEV), jax.random.fold_in(key_list[7], 1), 0, (V * (LEVELS // N_MEM) * COL_DEV) - 1).astype(jnp.int32)
    obs_value = noise(key_list[8], (OBS,), 1.0, 6.0, ((0, 32),), jnp.float32)
    obs_sigma = jnp.clip(jnp.exp(math.log(1.0) - 1.2039728 * jax.random.uniform(key_list[9], (OBS,), jnp.float32) ** shard_levels(key_list[9], (OBS,), ((0, 32),), -0.2, 0.2)), 0.3, 1.0)
    huber_mask = place_ends((jax.random.randint(key_list[10], (OBS,), 0, 4) < 3).astype(jnp.int32), jax.random.fold_in(key_list[10], 1), 0, 1)
    return {"control": control, "static_control_vector": static_control_vector, "perturb": perturb, "tiles": tiles, "block_offset": block_offset, "vert": vert, "static_vertical_root": static_vertical_root, "obs_index": obs_index, "obs_value": obs_value, "obs_sigma": obs_sigma, "huber_mask": huber_mask}


ENS_W = 0.85
STATIC_WEIGHT = 0.5
TAU = 0.5
HUBER_LOW = 0.3

def selectors(block_offset):
    count = block_offset.shape[0]
    blocks = jnp.arange(count, dtype=jnp.int32)
    source = (blocks[:, None] + block_offset) % count
    return (source.T[:, :, None] == blocks[None, None, :]).astype(jnp.float32)

def horizontal(field, tiles, picks):
    shaped = field.astype(jnp.float32).reshape(field.shape[:-1] + (NBLK, BLOCK))
    total = jnp.zeros(shaped.shape, jnp.float32)
    for slot in range(KNB):
        moved = jnp.einsum('bj,...jc->...bc', picks[slot], shaped, precision=lax.Precision.HIGHEST)
        total = total + jnp.einsum('...bc,cd->...bd', moved, tiles[slot].astype(jnp.float32), precision=lax.Precision.HIGHEST)
    return total.reshape(field.shape)

def horizontal_adjoint(field, tiles, picks):
    shaped = field.astype(jnp.float32).reshape(field.shape[:-1] + (NBLK, BLOCK))
    total = jnp.zeros(shaped.shape, jnp.float32)
    for slot in range(KNB):
        term = jnp.einsum('...bc,dc->...bd', shaped, tiles[slot].astype(jnp.float32), precision=lax.Precision.HIGHEST)
        total = total + jnp.einsum('bj,...bd->...jd', picks[slot], term, precision=lax.Precision.HIGHEST)
    return total.reshape(field.shape)

def to_blocks(field):
    shaped = field.reshape(V, N_MEM, LEVELS // N_MEM, N_LEV, COLS // N_LEV)
    return jnp.transpose(shaped, (3, 1, 0, 2, 4)).reshape(N_LEV * N_MEM, -1)

def from_blocks(blocks):
    shaped = blocks.reshape(N_LEV, N_MEM, V, LEVELS // N_MEM, COLS // N_LEV)
    return jnp.transpose(shaped, (2, 1, 3, 0, 4)).reshape(V, LEVELS, COLS)

def scatter_row(zeros_row, where_at, values):
    return zeros_row.at[where_at].add(values)

def reference(control, static_control_vector, perturb, tiles, block_offset, vert, static_vertical_root, obs_index, obs_value, obs_sigma, huber_mask):
    picks = selectors(block_offset)
    ens_gain = ENS_W / math.sqrt(M)
    weights = jnp.where(huber_mask == 1, jnp.float32(1.0), jnp.float32(HUBER_LOW))
    precision_obs = (weights / (obs_sigma * obs_sigma)).reshape(N_LEV * N_MEM, -1)
    where_obs = obs_index.reshape(N_LEV * N_MEM, -1).astype(jnp.int32)
    values_obs = obs_value.reshape(N_LEV * N_MEM, -1)
    vertical_forward = vert.astype(jnp.float32)
    static_forward = static_vertical_root.astype(jnp.float32)
    for turn in range(ITERS):
        local = lax.map(lambda member: horizontal(member, tiles, picks).astype(jnp.bfloat16), control)

        def accumulate(carry, pair):
            member_localized, member_pert = pair
            column_slice = jnp.einsum('tbu,tuo->tbo', vertical_forward, member_localized.astype(jnp.float32), precision=lax.Precision.HIGHEST)
            return (carry + column_slice * member_pert.astype(jnp.float32), None)
        ens, _ = lax.scan(accumulate, jnp.zeros((V, LEVELS, COLS), jnp.float32), (local, perturb))
        static_portion = jnp.einsum('tbu,tuo->tbo', static_forward, static_control_vector.astype(jnp.float32), precision=lax.Precision.HIGHEST)
        increment = ens_gain * ens + STATIC_WEIGHT * static_portion
        blocks = to_blocks(increment)
        seen = jnp.take_along_axis(blocks, where_obs, axis=1)
        resid = precision_obs * (seen - values_obs)
        grad_blocks = jax.vmap(scatter_row)(jnp.zeros_like(blocks), where_obs, resid)
        gradient_field_total = from_blocks(grad_blocks)
        static_gradient = static_control_vector.astype(jnp.float32) + STATIC_WEIGHT * jnp.einsum('otn,ote->one', static_forward, gradient_field_total, precision=lax.Precision.HIGHEST)

        def update(pair):
            member_ctl, member_pert = pair
            weighted_innovations = ens_gain * gradient_field_total * member_pert.astype(jnp.float32)
            backward_field = jnp.einsum('otn,ote->one', vertical_forward, weighted_innovations, precision=lax.Precision.HIGHEST).astype(jnp.bfloat16)
            adjoint = horizontal_adjoint(backward_field, tiles, picks)
            current = member_ctl.astype(jnp.float32)
            return (current - TAU * (current + adjoint)).astype(jnp.bfloat16)
        control = lax.map(update, (control, perturb))
        static_control_vector = (static_control_vector.astype(jnp.float32) - TAU * static_gradient).astype(jnp.bfloat16)
    return (control, static_control_vector)
```

```python
import functools
import math

import jax
import jax.numpy as jnp
from jax import lax
from jax.experimental import pallas as pl
from jax.experimental.pallas import tpu as pltpu
from jax.sharding import PartitionSpec as P

ITERS = 2


ENS_W = 0.85
STATIC_WEIGHT = 0.5
TAU = 0.5
HUBER_LOW = 0.3
MESH = pl.DeviceIdType.MESH


def selectors(block_offset):
    count = block_offset.shape[0]
    blocks = jnp.arange(count, dtype=jnp.int32)
    source = (blocks[:, None] + block_offset) % count
    return (source.T[:, :, None] == blocks[None, None, :]).astype(jnp.bfloat16)


def horizontal(field, tiles, picks):
    count = picks.shape[1]
    width = tiles.shape[1]
    shaped = field.reshape(field.shape[:-1] + (count, width))
    total = None
    for slot in range(tiles.shape[0]):
        moved = jnp.einsum(
            "bj,...jc->...bc", picks[slot], shaped, preferred_element_type=jnp.float32
        ).astype(jnp.bfloat16)
        term = jnp.einsum("...bc,cd->...bd", moved, tiles[slot], preferred_element_type=jnp.float32)
        total = term if total is None else total + term
    return total.reshape(field.shape).astype(jnp.bfloat16)


def horizontal_adjoint(field, tiles, picks):
    count = picks.shape[1]
    width = tiles.shape[1]
    shaped = field.reshape(field.shape[:-1] + (count, width))
    total = None
    for slot in range(tiles.shape[0]):
        term = jnp.einsum(
            "...bc,dc->...bd", shaped, tiles[slot], preferred_element_type=jnp.float32
        )
        moved = jnp.einsum(
            "bj,...bd->...jd",
            picks[slot].astype(jnp.float32),
            term,
            precision=lax.Precision.HIGHEST,
        )
        total = moved if total is None else total + moved
    return total.reshape(field.shape)


def observe(block, obs_index, obs_value, precision_obs):
    flat = block.reshape(-1)
    seen = flat[obs_index]
    resid = precision_obs * (seen - obs_value)
    return jnp.zeros_like(flat).at[obs_index].add(resid).reshape(block.shape)


def on_device(
    control,
    static_control_vector,
    perturb,
    tiles,
    block_offset,
    vert,
    static_vertical_root,
    obs_index,
    obs_value,
    obs_sigma,
    huber_mask,
):
    picks = selectors(block_offset)
    members_all = control.shape[0] * lax.axis_size("mem")
    ens_gain = ENS_W / math.sqrt(members_all)
    level_rows = static_control_vector.shape[1] // lax.axis_size("mem")
    first_level = lax.axis_index("mem") * level_rows
    weights = jnp.where(huber_mask == 1, jnp.float32(1.0), jnp.float32(HUBER_LOW))
    precision_obs = weights / (obs_sigma * obs_sigma)
    vertical_forward = vert.astype(jnp.float32)
    static_forward = static_vertical_root.astype(jnp.float32)
    for turn in range(ITERS):
        local = horizontal(control, tiles, picks)
        columns = lax.all_to_all(local, "lev", split_axis=3, concat_axis=2, tiled=True)
        vertical = jnp.einsum("vlk,mvkc->mvlc", vert, columns, preferred_element_type=jnp.float32)
        partial_value = jnp.sum(vertical * perturb.astype(jnp.float32), axis=0)
        static_portion = jnp.einsum(
            "tbu,tuo->tbo",
            static_vertical_root,
            static_control_vector,
            preferred_element_type=jnp.float32,
        )
        ens = lax.psum_scatter(partial_value, "mem", scatter_dimension=1, tiled=True)
        own_static = lax.dynamic_slice_in_dim(static_portion, first_level, level_rows, 1)
        increment = ens_gain * ens + STATIC_WEIGHT * own_static
        grad_block = observe(increment, obs_index, obs_value, precision_obs)
        gradient_field_total = lax.all_gather(grad_block, "mem", axis=1, tiled=True)
        static_gradient = static_control_vector.astype(jnp.float32) + STATIC_WEIGHT * jnp.einsum(
            "otn,ote->one", static_forward, gradient_field_total, precision=lax.Precision.HIGHEST
        )
        weighted_innovations = (ens_gain * gradient_field_total)[None] * perturb.astype(jnp.float32)
        backward_field = jnp.einsum(
            "vkl,mvkc->mvlc",
            vertical_forward,
            weighted_innovations,
            precision=lax.Precision.HIGHEST,
        ).astype(jnp.bfloat16)
        levels = lax.all_to_all(backward_field, "lev", split_axis=2, concat_axis=3, tiled=True)
        adjoint = horizontal_adjoint(levels, tiles, picks)
        current = control.astype(jnp.float32)
        control = (current - TAU * (current + adjoint)).astype(jnp.bfloat16)
        static_control_vector = (
            static_control_vector.astype(jnp.float32) - TAU * static_gradient
        ).astype(jnp.bfloat16)
    return (control, static_control_vector)


def split(value):
    high = value.astype(jnp.bfloat16)
    return high, (value - high.astype(jnp.float32)).astype(jnp.bfloat16)


def descent_kernel(
    ens_gain,
    control_ref,
    static_ref,
    perturb_ref,
    tiles_ref,
    offset_ref,
    vert_ref,
    root_ref,
    index_ref,
    value_ref,
    sigma_ref,
    mask_ref,
    control_out,
    static_out,
    dense,
    state,
    static_state,
    rows_in,
    inc0,
    inc,
    hot_row,
    hot_col,
    fwd_send,
    fwd_recv,
    sum_send,
    sum_recv,
    grad_recv,
    bwd_send,
    bwd_recv,
    send_sem,
    recv_sem,
):
    members, variables, per_lev, columns = control_ref.shape
    n_lev = lax.axis_size("lev")
    n_mem = lax.axis_size("mem")
    levels = vert_ref.shape[1]
    per_mem = levels // n_mem
    width = static_ref.shape[2]
    block = tiles_ref.shape[1]
    slots = tiles_ref.shape[0]
    count = columns // block
    chunk = members * per_lev
    my_lev = lax.axis_index("lev")
    my_mem = lax.axis_index("mem")

    barrier = pltpu.get_barrier_semaphore()
    for step in range(1, n_lev):
        pl.semaphore_signal(
            barrier, inc=1, device_id={"lev": lax.rem(my_lev + step, n_lev)}, device_id_type=MESH
        )
    for step in range(1, n_mem):
        pl.semaphore_signal(
            barrier, inc=1, device_id={"mem": lax.rem(my_mem + step, n_mem)}, device_id_type=MESH
        )

    lane = lax.broadcasted_iota(jnp.int32, (1, width), 1)
    wide = []
    for slot in range(slots):
        tile = tiles_ref[slot].astype(jnp.float32)
        wide.append(jnp.concatenate([tile] * (width // block), axis=1))
    sources = []
    for group in range(columns // width):
        per_slot = []
        for slot in range(slots):
            vec = jnp.zeros((1, width), jnp.int32)
            for part in range(width // block):
                b = group * (width // block) + part
                src = lax.rem(lax.rem(b + offset_ref[b, slot], count) + count, count)
                vec = jnp.where(lane >= part * block, src, vec)
            per_slot.append(vec)
        sources.append(per_slot)

    def build(j, carry):
        for group in range(columns // width):
            total = jnp.zeros((block, width), jnp.float32)
            for slot in range(slots):
                total = total + jnp.where(sources[group][slot] == j, wide[slot], 0.0)
            dense[pl.ds(pl.multiple_of(j * block, block), block), group * width : (group + 1) * width] = (
                total.astype(jnp.bfloat16)
            )
        return carry

    lax.fori_loop(0, count, build, 0)
    for v in range(variables):
        for m in range(members):
            state[v * chunk + m * per_lev : v * chunk + (m + 1) * per_lev, :] = control_ref[m, v]
    static_state[...] = static_ref[...]
    weights = jnp.where(mask_ref[...] == 1, jnp.float32(1.0), jnp.float32(HUBER_LOW))
    precision_obs = weights / (sigma_ref[...] * sigma_ref[...])
    pl.semaphore_wait(barrier, n_lev - 1 + n_mem - 1)

    def lev_copy(send, recv, turn, phase, v, peer):
        return pltpu.make_async_remote_copy(
            src_ref=send.at[turn, v, peer],
            dst_ref=recv.at[turn, v, my_lev],
            send_sem=send_sem.at[turn, phase, v],
            recv_sem=recv_sem.at[turn, phase, v],
            device_id={"lev": peer},
            device_id_type=MESH,
        )

    def mem_copy(src, dst, turn, phase, v, peer):
        return pltpu.make_async_remote_copy(
            src_ref=src,
            dst_ref=dst,
            send_sem=send_sem.at[turn, phase, v],
            recv_sem=recv_sem.at[turn, phase, v],
            device_id={"mem": peer},
            device_id_type=MESH,
        )

    def await_blocks(buffer, sem, turn, phase, v, blocks):
        part = buffer.at[turn, v, pl.ds(0, blocks)]
        pltpu.make_async_copy(part, part, sem.at[turn, phase, v]).wait()

    def one_turn(turn, carry):
        half = 2 * width
        for pair in range(columns // half):
            local = jnp.dot(
                state[...],
                dense[:, pair * half : (pair + 1) * half],
                preferred_element_type=jnp.float32,
            ).astype(jnp.bfloat16)
            for v in range(variables):
                for side in range(2):
                    fwd_send[turn, v, pair * 2 + side] = local[
                        v * chunk : (v + 1) * chunk, side * width : (side + 1) * width
                    ]
        for v in range(variables):
            for step in range(1, n_lev):
                lev_copy(fwd_send, fwd_recv, turn, 0, v, lax.rem(my_lev + step, n_lev)).start()
        for v in range(variables):
            fwd_recv[turn, v, my_lev] = fwd_send[turn, v, my_lev]

        first = pl.multiple_of(my_mem * per_mem, per_mem)
        for v in range(variables):
            inc0[v * per_mem : (v + 1) * per_mem, :] = STATIC_WEIGHT * jnp.dot(
                root_ref[v, pl.ds(first, per_mem), :],
                static_state[v],
                preferred_element_type=jnp.float32,
            )
        where_obs = index_ref[...]
        row_of = where_obs // width
        col_of = where_obs - row_of * width
        observations = where_obs.shape[1]
        hot_row[...] = jnp.where(
            lax.broadcasted_iota(jnp.int32, (variables * per_mem, observations), 0) == row_of, 1.0, 0.0
        ).astype(jnp.bfloat16)
        hot_col[...] = jnp.where(
            lax.broadcasted_iota(jnp.int32, (width, observations), 0) == col_of, 1.0, 0.0
        )

        for v in range(variables):
            await_blocks(fwd_recv, recv_sem, turn, 0, v, n_lev - 1)
            cols = [
                fwd_recv[turn, v, :, m * per_lev : (m + 1) * per_lev, :].reshape(levels, width)
                for m in range(members)
            ]
            vertical = jnp.dot(
                vert_ref[v], jnp.concatenate(cols, axis=1), preferred_element_type=jnp.float32
            )
            total = None
            for m in range(members):
                term = vertical[:, m * width : (m + 1) * width] * perturb_ref[m, v].astype(jnp.float32)
                total = term if total is None else total + term
            sum_send[turn, v] = total.reshape(n_mem, per_mem, width)
            for step in range(1, n_mem):
                peer = lax.rem(my_mem + step, n_mem)
                mem_copy(
                    sum_send.at[turn, v, peer], sum_recv.at[turn, v, my_mem], turn, 1, v, peer
                ).start()
            sum_recv[turn, v, my_mem] = sum_send[turn, v, my_mem]
        for v in range(variables):
            await_blocks(sum_recv, recv_sem, turn, 1, v, n_mem - 1)
            ens = jnp.sum(sum_recv[turn, v], axis=0)
            own = slice(v * per_mem, (v + 1) * per_mem)
            inc[own, :] = ens_gain * ens + inc0[own, :]

        high, low = split(inc[...])
        picked = lax.dot_general(
            jnp.concatenate([high, low], axis=1),
            hot_row[...],
            (((0,), (0,)), ((), ())),
            preferred_element_type=jnp.float32,
        )
        seen = jnp.sum(
            (picked[:width] + picked[width:]) * hot_col[...], axis=0, keepdims=True
        )
        resid = precision_obs * (seen - value_ref[...])
        high, low = split(hot_col[...] * resid)
        spread = lax.dot_general(
            hot_row[...],
            jnp.concatenate([high, low], axis=0),
            (((1,), (1,)), ((), ())),
            preferred_element_type=jnp.float32,
        )
        grad = spread[:, :width] + spread[:, width:]
        for v in range(variables):
            grad_recv[turn, v, my_mem] = grad[v * per_mem : (v + 1) * per_mem, :]
            for step in range(1, n_mem):
                peer = lax.rem(my_mem + step, n_mem)
                mem_copy(
                    grad_recv.at[turn, v, my_mem], grad_recv.at[turn, v, my_mem], turn, 2, v, peer
                ).start()

        for v in range(variables):
            await_blocks(grad_recv, recv_sem, turn, 2, v, n_mem - 1)
            field = grad_recv[turn, v].reshape(levels, width)
            parts = [
                split((ens_gain * field) * perturb_ref[m, v].astype(jnp.float32))
                for m in range(members)
            ]
            product = lax.dot_general(
                vert_ref[v],
                jnp.concatenate([p[0] for p in parts] + [p[1] for p in parts], axis=1),
                (((0,), (0,)), ((), ())),
                preferred_element_type=jnp.float32,
            )
            back = product[:, : members * width] + product[:, members * width :]
            for m in range(members):
                bwd_send[turn, v, :, m * per_lev : (m + 1) * per_lev, :] = (
                    back[:, m * width : (m + 1) * width]
                    .astype(jnp.bfloat16)
                    .reshape(n_lev, per_lev, width)
                )
            for step in range(1, n_lev):
                lev_copy(bwd_send, bwd_recv, turn, 3, v, lax.rem(my_lev + step, n_lev)).start()
            bwd_recv[turn, v, my_lev] = bwd_send[turn, v, my_lev]

        for v in range(variables):
            high, low = split(grad_recv[turn, v].reshape(levels, width))
            product = lax.dot_general(
                root_ref[v],
                jnp.concatenate([high, low], axis=1),
                (((0,), (0,)), ((), ())),
                preferred_element_type=jnp.float32,
            )
            current = static_state[v].astype(jnp.float32)
            gradient = current + STATIC_WEIGHT * (product[:, :width] + product[:, width:])
            static_state[v] = (current - TAU * gradient).astype(jnp.bfloat16)

        for v in range(variables):
            await_blocks(bwd_recv, recv_sem, turn, 3, v, n_lev - 1)
            for peer in range(n_lev):
                rows_in[v * chunk : (v + 1) * chunk, peer * width : (peer + 1) * width] = bwd_recv[
                    turn, v, peer
                ]
        for pair in range(columns // half):
            here = slice(pair * half, (pair + 1) * half)
            adjoint = lax.dot_general(
                rows_in[...],
                dense[here, :],
                (((1,), (1,)), ((), ())),
                preferred_element_type=jnp.float32,
            )
            current = state[:, here].astype(jnp.float32)
            state[:, here] = (current - TAU * (current + adjoint)).astype(jnp.bfloat16)
        return carry

    lax.fori_loop(0, ITERS, one_turn, 0)
    for v in range(variables):
        for m in range(members):
            control_out[m, v] = state[v * chunk + m * per_lev : v * chunk + (m + 1) * per_lev, :]
    static_out[...] = static_state[...]

    def drain(turn, carry):
        for v in range(variables):
            await_blocks(fwd_send, send_sem, turn, 0, v, n_lev - 1)
            await_blocks(sum_send, send_sem, turn, 1, v, n_mem - 1)
            await_blocks(grad_recv, send_sem, turn, 2, v, n_mem - 1)
            await_blocks(bwd_send, send_sem, turn, 3, v, n_lev - 1)
        return carry

    lax.fori_loop(0, ITERS, drain, 0)


def fused(
    control,
    static_control_vector,
    perturb,
    tiles,
    block_offset,
    vert,
    static_vertical_root,
    obs_index,
    obs_value,
    obs_sigma,
    huber_mask,
):
    members, variables, per_lev, columns = control.shape
    n_lev, n_mem = lax.axis_size("lev"), lax.axis_size("mem")
    levels, width = static_control_vector.shape[1:]
    per_mem = levels // n_mem
    chunk = members * per_lev
    observations = obs_index.shape[0]
    rows = variables * chunk
    ens_gain = ENS_W / math.sqrt(members * n_mem)
    vmem = pl.BlockSpec(memory_space=pltpu.VMEM)
    lev_buffer = pltpu.VMEM((ITERS, variables, n_lev, chunk, width), jnp.bfloat16)
    mem_buffer = pltpu.VMEM((ITERS, variables, n_mem, per_mem, width), jnp.float32)
    in_specs = [vmem] * 11
    in_specs[4] = pl.BlockSpec(memory_space=pltpu.SMEM)
    flat = (1, observations)
    return pl.pallas_call(
        functools.partial(descent_kernel, ens_gain),
        out_shape=(
            jax.ShapeDtypeStruct(control.shape, control.dtype),
            jax.ShapeDtypeStruct(static_control_vector.shape, static_control_vector.dtype),
        ),
        in_specs=in_specs,
        out_specs=(vmem, vmem),
        scratch_shapes=[
            pltpu.VMEM((columns, columns), jnp.bfloat16),
            pltpu.VMEM((rows, columns), jnp.bfloat16),
            pltpu.VMEM((variables, levels, width), jnp.bfloat16),
            pltpu.VMEM((rows, columns), jnp.bfloat16),
            pltpu.VMEM((variables * per_mem, width), jnp.float32),
            pltpu.VMEM((variables * per_mem, width), jnp.float32),
            pltpu.VMEM((variables * per_mem, observations), jnp.bfloat16),
            pltpu.VMEM((width, observations), jnp.float32),
            lev_buffer,
            lev_buffer,
            mem_buffer,
            mem_buffer,
            mem_buffer,
            lev_buffer,
            lev_buffer,
            pltpu.SemaphoreType.DMA((ITERS, 4, variables)),
            pltpu.SemaphoreType.DMA((ITERS, 4, variables)),
        ],
        compiler_params=pltpu.CompilerParams(
            collective_id=0, has_side_effects=True, vmem_limit_bytes=40 * 1024 * 1024
        ),
    )(
        control,
        static_control_vector,
        perturb,
        tiles,
        block_offset,
        vert,
        static_vertical_root,
        obs_index.reshape(flat),
        obs_value.reshape(flat),
        obs_sigma.reshape(flat),
        huber_mask.reshape(flat),
    )


def suits(control, static_control_vector, tiles):
    per_lev, columns = control.shape[2:]
    levels, width = static_control_vector.shape[1:]
    return (
        per_lev % 16 == 0
        and width % 128 == 0
        and columns % (2 * width) == 0
        and width % tiles.shape[1] == 0
        and (levels // lax.axis_size("mem")) % 16 == 0
        and columns <= 2048
    )


def descent(*arguments):
    if suits(arguments[0], arguments[1], arguments[3]):
        return fused(*arguments)
    return on_device(*arguments)


def solution(mesh):
    placed = (
        P("mem", None, "lev", None),
        P(None, None, "lev"),
        P("mem", None, None, "lev"),
        P(),
        P(),
        P(),
        P(),
        P(("lev", "mem")),
        P(("lev", "mem")),
        P(("lev", "mem")),
        P(("lev", "mem")),
    )
    return jax.shard_map(
        descent,
        mesh=mesh,
        in_specs=placed,
        out_specs=(P("mem", None, "lev", None), P(None, None, "lev")),
        check_vma=False,
    )
```

```python
import functools
import math

import jax
import jax.numpy as jnp
from jax import lax
from jax.experimental import pallas as pl
from jax.experimental.pallas import tpu as pltpu
from jax.sharding import PartitionSpec as P

ITERS = 2


ENS_W = 0.85
STATIC_WEIGHT = 0.5
TAU = 0.5
HUBER_LOW = 0.3
MESH = pl.DeviceIdType.MESH


def selectors(block_offset):
    count = block_offset.shape[0]
    blocks = jnp.arange(count, dtype=jnp.int32)
    source = (blocks[:, None] + block_offset) % count
    return (source.T[:, :, None] == blocks[None, None, :]).astype(jnp.bfloat16)


def horizontal(field, tiles, picks):
    count = picks.shape[1]
    width = tiles.shape[1]
    shaped = field.reshape(field.shape[:-1] + (count, width))
    total = None
    for slot in range(tiles.shape[0]):
        moved = jnp.einsum(
            "bj,...jc->...bc", picks[slot], shaped, preferred_element_type=jnp.float32
        ).astype(jnp.bfloat16)
        term = jnp.einsum("...bc,cd->...bd", moved, tiles[slot], preferred_element_type=jnp.float32)
        total = term if total is None else total + term
    return total.reshape(field.shape).astype(jnp.bfloat16)


def horizontal_adjoint(field, tiles, picks):
    count = picks.shape[1]
    width = tiles.shape[1]
    shaped = field.reshape(field.shape[:-1] + (count, width))
    total = None
    for slot in range(tiles.shape[0]):
        term = jnp.einsum(
            "...bc,dc->...bd", shaped, tiles[slot], preferred_element_type=jnp.float32
        )
        moved = jnp.einsum(
            "bj,...bd->...jd",
            picks[slot].astype(jnp.float32),
            term,
            precision=lax.Precision.HIGHEST,
        )
        total = moved if total is None else total + moved
    return total.reshape(field.shape)


def observe(block, obs_index, obs_value, precision_obs):
    flat = block.reshape(-1)
    seen = flat[obs_index]
    resid = precision_obs * (seen - obs_value)
    return jnp.zeros_like(flat).at[obs_index].add(resid).reshape(block.shape)


def on_device(
    control,
    static_control_vector,
    perturb,
    tiles,
    block_offset,
    vert,
    static_vertical_root,
    obs_index,
    obs_value,
    obs_sigma,
    huber_mask,
):
    picks = selectors(block_offset)
    members_all = control.shape[0] * lax.axis_size("mem")
    ens_gain = ENS_W / math.sqrt(members_all)
    level_rows = static_control_vector.shape[1] // lax.axis_size("mem")
    first_level = lax.axis_index("mem") * level_rows
    weights = jnp.where(huber_mask == 1, jnp.float32(1.0), jnp.float32(HUBER_LOW))
    precision_obs = weights / (obs_sigma * obs_sigma)
    vertical_forward = vert.astype(jnp.float32)
    static_forward = static_vertical_root.astype(jnp.float32)
    for turn in range(ITERS):
        local = horizontal(control, tiles, picks)
        columns = lax.all_to_all(local, "lev", split_axis=3, concat_axis=2, tiled=True)
        vertical = jnp.einsum("vlk,mvkc->mvlc", vert, columns, preferred_element_type=jnp.float32)
        partial_value = jnp.sum(vertical * perturb.astype(jnp.float32), axis=0)
        static_portion = jnp.einsum(
            "tbu,tuo->tbo",
            static_vertical_root,
            static_control_vector,
            preferred_element_type=jnp.float32,
        )
        ens = lax.psum_scatter(partial_value, "mem", scatter_dimension=1, tiled=True)
        own_static = lax.dynamic_slice_in_dim(static_portion, first_level, level_rows, 1)
        increment = ens_gain * ens + STATIC_WEIGHT * own_static
        grad_block = observe(increment, obs_index, obs_value, precision_obs)
        gradient_field_total = lax.all_gather(grad_block, "mem", axis=1, tiled=True)
        static_gradient = static_control_vector.astype(jnp.float32) + STATIC_WEIGHT * jnp.einsum(
            "otn,ote->one", static_forward, gradient_field_total, precision=lax.Precision.HIGHEST
        )
        weighted_innovations = (ens_gain * gradient_field_total)[None] * perturb.astype(jnp.float32)
        backward_field = jnp.einsum(
            "vkl,mvkc->mvlc",
            vertical_forward,
            weighted_innovations,
            precision=lax.Precision.HIGHEST,
        ).astype(jnp.bfloat16)
        levels = lax.all_to_all(backward_field, "lev", split_axis=2, concat_axis=3, tiled=True)
        adjoint = horizontal_adjoint(levels, tiles, picks)
        current = control.astype(jnp.float32)
        control = (current - TAU * (current + adjoint)).astype(jnp.bfloat16)
        static_control_vector = (
            static_control_vector.astype(jnp.float32) - TAU * static_gradient
        ).astype(jnp.bfloat16)
    return (control, static_control_vector)


def split(value):
    high = value.astype(jnp.bfloat16)
    return high, (value - high.astype(jnp.float32)).astype(jnp.bfloat16)


def descent_kernel(
    ens_gain,
    control_hbm,
    static_hbm,
    perturb_hbm,
    tiles_hbm,
    offset_ref,
    vert_hbm,
    root_hbm,
    index_hbm,
    value_hbm,
    sigma_hbm,
    mask_hbm,
    control_out,
    static_out,
    perturb_ref,
    tiles_ref,
    vert_ref,
    root_ref,
    index_ref,
    value_ref,
    sigma_ref,
    mask_ref,
    dense,
    state,
    static_state,
    rows_in,
    inc0,
    precision_obs,
    hot_row,
    hot_col,
    fwd_send,
    fwd_recv,
    sum_send,
    sum_recv,
    grad_recv,
    bwd_send,
    bwd_recv,
    send_sem,
    recv_sem,
    fetch_sem,
):
    members, variables, per_lev, columns = control_hbm.shape
    n_lev = lax.axis_size("lev")
    n_mem = lax.axis_size("mem")
    levels = vert_ref.shape[1]
    per_mem = levels // n_mem
    width = static_state.shape[2]
    block = tiles_ref.shape[1]
    slots = tiles_ref.shape[0]
    count = columns // block
    chunk = members * per_lev
    my_lev = lax.axis_index("lev")
    my_mem = lax.axis_index("mem")

    barrier = pltpu.get_barrier_semaphore()
    for step in range(1, n_lev):
        pl.semaphore_signal(
            barrier, inc=1, device_id={"lev": lax.rem(my_lev + step, n_lev)}, device_id_type=MESH
        )
    for step in range(1, n_mem):
        pl.semaphore_signal(
            barrier, inc=1, device_id={"mem": lax.rem(my_mem + step, n_mem)}, device_id_type=MESH
        )

    tiles_copy = pltpu.make_async_copy(tiles_hbm, tiles_ref, fetch_sem.at[0])
    tiles_copy.start()
    for v in range(variables):
        for m in range(members):
            pltpu.make_async_copy(
                control_hbm.at[m, v],
                state.at[pl.ds(v * chunk + m * per_lev, per_lev)],
                fetch_sem.at[1],
            ).start()
    late = []
    for place, (source, target) in enumerate(
        (
            (root_hbm, root_ref),
            (static_hbm, static_state),
            (index_hbm, index_ref),
            (vert_hbm, vert_ref),
            (perturb_hbm, perturb_ref),
            (value_hbm, value_ref),
            (sigma_hbm, sigma_ref),
            (mask_hbm, mask_ref),
        )
    ):
        late.append(pltpu.make_async_copy(source, target, fetch_sem.at[2 + place]))
        late[-1].start()
    tiles_copy.wait()

    lane = lax.broadcasted_iota(jnp.int32, (1, width), 1)
    wide = []
    for slot in range(slots):
        tile = tiles_ref[slot].astype(jnp.float32)
        wide.append(jnp.concatenate([tile] * (width // block), axis=1))
    sources = []
    for group in range(columns // width):
        per_slot = []
        for slot in range(slots):
            vec = jnp.zeros((1, width), jnp.int32)
            for part in range(width // block):
                b = group * (width // block) + part
                src = lax.rem(lax.rem(b + offset_ref[slot, b], count) + count, count)
                vec = jnp.where(lane >= part * block, src, vec)
            per_slot.append(vec)
        sources.append(per_slot)

    def build(j, carry):
        for group in range(columns // width):
            total = jnp.zeros((block, width), jnp.float32)
            for slot in range(slots):
                total = total + jnp.where(sources[group][slot] == j, wide[slot], 0.0)
            dense[pl.ds(pl.multiple_of(j * block, block), block), group * width : (group + 1) * width] = (
                total.astype(jnp.bfloat16)
            )
        return carry

    lax.fori_loop(0, count, build, 0)
    pltpu.make_async_copy(state, state, fetch_sem.at[1]).wait()
    pl.semaphore_wait(barrier, n_lev - 1 + n_mem - 1)

    def lev_copy(send, recv, turn, phase, v, peer):
        return pltpu.make_async_remote_copy(
            src_ref=send.at[turn, v, peer],
            dst_ref=recv.at[turn, v, my_lev],
            send_sem=send_sem.at[turn, phase, v],
            recv_sem=recv_sem.at[turn, phase, v],
            device_id={"lev": peer},
            device_id_type=MESH,
        )

    def mem_copy(src, dst, turn, phase, v, peer):
        return pltpu.make_async_remote_copy(
            src_ref=src,
            dst_ref=dst,
            send_sem=send_sem.at[turn, phase, v],
            recv_sem=recv_sem.at[turn, phase, v],
            device_id={"mem": peer},
            device_id_type=MESH,
        )

    def await_blocks(buffer, sem, turn, phase, v, blocks):
        part = buffer.at[turn, v, pl.ds(0, blocks)]
        pltpu.make_async_copy(part, part, sem.at[turn, phase, v]).wait()

    half = 2 * width
    cut = (variables + 1) // 2
    groups = [g for g in (range(cut), range(cut, variables)) if len(g)]

    def forward(turn, group):
        rows = slice(group[0] * chunk, (group[-1] + 1) * chunk)
        for pair in range(columns // half):
            local = jnp.dot(
                state[rows, :],
                dense[:, pair * half : (pair + 1) * half],
                preferred_element_type=jnp.float32,
            ).astype(jnp.bfloat16)
            for place, v in enumerate(group):
                for side in range(2):
                    fwd_send[turn, v, pair * 2 + side] = local[
                        place * chunk : (place + 1) * chunk, side * width : (side + 1) * width
                    ]
        for v in group:
            for step in range(1, n_lev):
                lev_copy(fwd_send, fwd_recv, turn, 0, v, lax.rem(my_lev + step, n_lev)).start()
        for v in group:
            fwd_recv[turn, v, my_lev] = fwd_send[turn, v, my_lev]

    def static_forward():
        first = pl.multiple_of(my_mem * per_mem, per_mem)
        for v in range(variables):
            inc0[v * per_mem : (v + 1) * per_mem, :] = STATIC_WEIGHT * jnp.dot(
                root_ref[v, pl.ds(first, per_mem), :],
                static_state[v],
                preferred_element_type=jnp.float32,
            )

    def member_sum(turn, v):
        await_blocks(fwd_recv, recv_sem, turn, 0, v, n_lev - 1)
        cols = [
            fwd_recv[turn, v, :, m * per_lev : (m + 1) * per_lev, :].reshape(levels, width)
            for m in range(members)
        ]
        vertical = jnp.dot(
            vert_ref[v], jnp.concatenate(cols, axis=1), preferred_element_type=jnp.float32
        )
        total = None
        for m in range(members):
            term = vertical[:, m * width : (m + 1) * width] * perturb_ref[m, v].astype(jnp.float32)
            total = term if total is None else total + term
        sum_send[turn, v] = total.reshape(n_mem, per_mem, width)
        for step in range(1, n_mem):
            peer = lax.rem(my_mem + step, n_mem)
            mem_copy(
                sum_send.at[turn, v, peer], sum_recv.at[turn, v, my_mem], turn, 1, v, peer
            ).start()
        sum_recv[turn, v, my_mem] = sum_send[turn, v, my_mem]

    def observe_one(turn, v):
        await_blocks(sum_recv, recv_sem, turn, 1, v, n_mem - 1)
        own = slice(v * per_mem, (v + 1) * per_mem)
        increment = ens_gain * jnp.sum(sum_recv[turn, v], axis=0) + inc0[own, :]
        high, low = split(increment)
        picked = lax.dot_general(
            jnp.concatenate([high, low], axis=1),
            hot_row[own, :],
            (((0,), (0,)), ((), ())),
            preferred_element_type=jnp.float32,
        )
        seen = jnp.sum((picked[:width] + picked[width:]) * hot_col[...], axis=0, keepdims=True)
        resid = precision_obs[...] * (seen - value_ref[...])
        high, low = split(hot_col[...] * resid)
        spread = lax.dot_general(
            hot_row[own, :],
            jnp.concatenate([high, low], axis=0),
            (((1,), (1,)), ((), ())),
            preferred_element_type=jnp.float32,
        )
        grad_recv[turn, v, my_mem] = spread[:, :width] + spread[:, width:]
        for step in range(1, n_mem):
            peer = lax.rem(my_mem + step, n_mem)
            mem_copy(
                grad_recv.at[turn, v, my_mem], grad_recv.at[turn, v, my_mem], turn, 2, v, peer
            ).start()

    def vertical_adjoint(turn, v):
        await_blocks(grad_recv, recv_sem, turn, 2, v, n_mem - 1)
        field = grad_recv[turn, v].reshape(levels, width)
        parts = [
            split((ens_gain * field) * perturb_ref[m, v].astype(jnp.float32)) for m in range(members)
        ]
        product = lax.dot_general(
            vert_ref[v],
            jnp.concatenate([p[0] for p in parts] + [p[1] for p in parts], axis=1),
            (((0,), (0,)), ((), ())),
            preferred_element_type=jnp.float32,
        )
        back = product[:, : members * width] + product[:, members * width :]
        for m in range(members):
            bwd_send[turn, v, :, m * per_lev : (m + 1) * per_lev, :] = (
                back[:, m * width : (m + 1) * width]
                .astype(jnp.bfloat16)
                .reshape(n_lev, per_lev, width)
            )
        for step in range(1, n_lev):
            lev_copy(bwd_send, bwd_recv, turn, 3, v, lax.rem(my_lev + step, n_lev)).start()
        bwd_recv[turn, v, my_lev] = bwd_send[turn, v, my_lev]

    def static_update(turn):
        for v in range(variables):
            high, low = split(grad_recv[turn, v].reshape(levels, width))
            product = lax.dot_general(
                root_ref[v],
                jnp.concatenate([high, low], axis=1),
                (((0,), (0,)), ((), ())),
                preferred_element_type=jnp.float32,
            )
            current = static_state[v].astype(jnp.float32)
            gradient = current + STATIC_WEIGHT * (product[:, :width] + product[:, width:])
            static_state[v] = (current - TAU * gradient).astype(jnp.bfloat16)

    def horizontal_update(turn, group):
        rows = slice(group[0] * chunk, (group[-1] + 1) * chunk)
        for v in group:
            await_blocks(bwd_recv, recv_sem, turn, 3, v, n_lev - 1)
            for peer in range(n_lev):
                rows_in[v * chunk : (v + 1) * chunk, peer * width : (peer + 1) * width] = bwd_recv[
                    turn, v, peer
                ]
        for pair in range(columns // half):
            here = slice(pair * half, (pair + 1) * half)
            adjoint = lax.dot_general(
                rows_in[rows, :],
                dense[here, :],
                (((1,), (1,)), ((), ())),
                preferred_element_type=jnp.float32,
            )
            current = state[rows, here].astype(jnp.float32)
            state[rows, here] = (current - TAU * (current + adjoint)).astype(jnp.bfloat16)

    for group in groups:
        forward(0, group)
    for copy in late:
        copy.wait()
    static_forward()
    where_obs = index_ref[...]
    row_of = where_obs // width
    col_of = where_obs - row_of * width
    hot_row[...] = jnp.where(
        lax.broadcasted_iota(jnp.int32, hot_row.shape, 0) == row_of, 1.0, 0.0
    ).astype(jnp.bfloat16)
    hot_col[...] = jnp.where(lax.broadcasted_iota(jnp.int32, hot_col.shape, 0) == col_of, 1.0, 0.0)
    weights = jnp.where(mask_ref[...] == 1, jnp.float32(1.0), jnp.float32(HUBER_LOW))
    precision_obs[...] = weights / (sigma_ref[...] * sigma_ref[...])

    for turn in range(ITERS):
        for tick in range(variables + 4):
            if tick < variables:
                member_sum(turn, tick)
            if 0 <= tick - 2 < variables:
                observe_one(turn, tick - 2)
            if 0 <= tick - 4 < variables:
                vertical_adjoint(turn, tick - 4)
        static_update(turn)
        if turn + 1 < ITERS:
            static_forward()
        for group in groups:
            horizontal_update(turn, group)
            if turn + 1 < ITERS:
                forward(turn + 1, group)

    for v in range(variables):
        for m in range(members):
            control_out[m, v] = state[v * chunk + m * per_lev : v * chunk + (m + 1) * per_lev, :]
    static_out[...] = static_state[...]

    def drain(turn, carry):
        for v in range(variables):
            await_blocks(fwd_send, send_sem, turn, 0, v, n_lev - 1)
            await_blocks(sum_send, send_sem, turn, 1, v, n_mem - 1)
            await_blocks(grad_recv, send_sem, turn, 2, v, n_mem - 1)
            await_blocks(bwd_send, send_sem, turn, 3, v, n_lev - 1)
        return carry

    lax.fori_loop(0, ITERS, drain, 0)


def fused(
    control,
    static_control_vector,
    perturb,
    tiles,
    block_offset,
    vert,
    static_vertical_root,
    obs_index,
    obs_value,
    obs_sigma,
    huber_mask,
):
    members, variables, per_lev, columns = control.shape
    n_lev, n_mem = lax.axis_size("lev"), lax.axis_size("mem")
    levels, width = static_control_vector.shape[1:]
    per_mem = levels // n_mem
    chunk = members * per_lev
    observations = obs_index.shape[0]
    rows = variables * chunk
    ens_gain = ENS_W / math.sqrt(members * n_mem)
    vmem = pl.BlockSpec(memory_space=pltpu.VMEM)
    lev_buffer = pltpu.VMEM((ITERS, variables, n_lev, chunk, width), jnp.bfloat16)
    mem_buffer = pltpu.VMEM((ITERS, variables, n_mem, per_mem, width), jnp.float32)
    in_specs = [pl.BlockSpec(memory_space=pl.ANY)] * 11
    in_specs[4] = pl.BlockSpec(memory_space=pltpu.SMEM)
    flat = (1, observations)
    return pl.pallas_call(
        functools.partial(descent_kernel, ens_gain),
        out_shape=(
            jax.ShapeDtypeStruct(control.shape, control.dtype),
            jax.ShapeDtypeStruct(static_control_vector.shape, static_control_vector.dtype),
        ),
        in_specs=in_specs,
        out_specs=(vmem, vmem),
        scratch_shapes=[
            pltpu.VMEM(perturb.shape, perturb.dtype),
            pltpu.VMEM(tiles.shape, tiles.dtype),
            pltpu.VMEM(vert.shape, vert.dtype),
            pltpu.VMEM(static_vertical_root.shape, static_vertical_root.dtype),
            pltpu.VMEM(flat, obs_index.dtype),
            pltpu.VMEM(flat, obs_value.dtype),
            pltpu.VMEM(flat, obs_sigma.dtype),
            pltpu.VMEM(flat, huber_mask.dtype),
            pltpu.VMEM((columns, columns), jnp.bfloat16),
            pltpu.VMEM((rows, columns), jnp.bfloat16),
            pltpu.VMEM((variables, levels, width), jnp.bfloat16),
            pltpu.VMEM((rows, columns), jnp.bfloat16),
            pltpu.VMEM((variables * per_mem, width), jnp.float32),
            pltpu.VMEM(flat, jnp.float32),
            pltpu.VMEM((variables * per_mem, observations), jnp.bfloat16),
            pltpu.VMEM((width, observations), jnp.float32),
            lev_buffer,
            lev_buffer,
            mem_buffer,
            mem_buffer,
            mem_buffer,
            lev_buffer,
            lev_buffer,
            pltpu.SemaphoreType.DMA((ITERS, 4, variables)),
            pltpu.SemaphoreType.DMA((ITERS, 4, variables)),
            pltpu.SemaphoreType.DMA((10,)),
        ],
        compiler_params=pltpu.CompilerParams(
            collective_id=0, has_side_effects=True, vmem_limit_bytes=60 * 1024 * 1024
        ),
    )(
        control,
        static_control_vector,
        perturb,
        tiles,
        block_offset.T,
        vert,
        static_vertical_root,
        obs_index.reshape(flat),
        obs_value.reshape(flat),
        obs_sigma.reshape(flat),
        huber_mask.reshape(flat),
    )


def suits(control, static_control_vector, tiles):
    per_lev, columns = control.shape[2:]
    levels, width = static_control_vector.shape[1:]
    return (
        per_lev % 16 == 0
        and width % 128 == 0
        and columns % (2 * width) == 0
        and width % tiles.shape[1] == 0
        and (levels // lax.axis_size("mem")) % 16 == 0
        and columns <= 2048
    )


def descent(*arguments):
    if suits(arguments[0], arguments[1], arguments[3]):
        return fused(*arguments)
    return on_device(*arguments)


def solution(mesh):
    placed = (
        P("mem", None, "lev", None),
        P(None, None, "lev"),
        P("mem", None, None, "lev"),
        P(),
        P(),
        P(),
        P(),
        P(("lev", "mem")),
        P(("lev", "mem")),
        P(("lev", "mem")),
        P(("lev", "mem")),
    )
    return jax.shard_map(
        descent,
        mesh=mesh,
        in_specs=placed,
        out_specs=(P("mem", None, "lev", None), P(None, None, "lev")),
        check_vma=False,
    )
```

```python
import functools
import math

import jax
import jax.numpy as jnp
from jax import lax
from jax.experimental import pallas as pl
from jax.experimental.pallas import tpu as pltpu
from jax.sharding import PartitionSpec as P

ITERS = 2


ENS_W = 0.85
STATIC_WEIGHT = 0.5
TAU = 0.5
HUBER_LOW = 0.3
MESH = pl.DeviceIdType.MESH


def selectors(block_offset):
    count = block_offset.shape[0]
    blocks = jnp.arange(count, dtype=jnp.int32)
    source = (blocks[:, None] + block_offset) % count
    return (source.T[:, :, None] == blocks[None, None, :]).astype(jnp.bfloat16)


def horizontal(field, tiles, picks):
    count = picks.shape[1]
    width = tiles.shape[1]
    shaped = field.reshape(field.shape[:-1] + (count, width))
    total = None
    for slot in range(tiles.shape[0]):
        moved = jnp.einsum(
            "bj,...jc->...bc", picks[slot], shaped, preferred_element_type=jnp.float32
        ).astype(jnp.bfloat16)
        term = jnp.einsum("...bc,cd->...bd", moved, tiles[slot], preferred_element_type=jnp.float32)
        total = term if total is None else total + term
    return total.reshape(field.shape).astype(jnp.bfloat16)


def horizontal_adjoint(field, tiles, picks):
    count = picks.shape[1]
    width = tiles.shape[1]
    shaped = field.reshape(field.shape[:-1] + (count, width))
    total = None
    for slot in range(tiles.shape[0]):
        term = jnp.einsum(
            "...bc,dc->...bd", shaped, tiles[slot], preferred_element_type=jnp.float32
        )
        moved = jnp.einsum(
            "bj,...bd->...jd",
            picks[slot].astype(jnp.float32),
            term,
            precision=lax.Precision.HIGHEST,
        )
        total = moved if total is None else total + moved
    return total.reshape(field.shape)


def observe(block, obs_index, obs_value, precision_obs):
    flat = block.reshape(-1)
    seen = flat[obs_index]
    resid = precision_obs * (seen - obs_value)
    return jnp.zeros_like(flat).at[obs_index].add(resid).reshape(block.shape)


def on_device(
    control,
    static_control_vector,
    perturb,
    tiles,
    block_offset,
    vert,
    static_vertical_root,
    obs_index,
    obs_value,
    obs_sigma,
    huber_mask,
):
    picks = selectors(block_offset)
    members_all = control.shape[0] * lax.axis_size("mem")
    ens_gain = ENS_W / math.sqrt(members_all)
    level_rows = static_control_vector.shape[1] // lax.axis_size("mem")
    first_level = lax.axis_index("mem") * level_rows
    weights = jnp.where(huber_mask == 1, jnp.float32(1.0), jnp.float32(HUBER_LOW))
    precision_obs = weights / (obs_sigma * obs_sigma)
    vertical_forward = vert.astype(jnp.float32)
    static_forward = static_vertical_root.astype(jnp.float32)
    for turn in range(ITERS):
        local = horizontal(control, tiles, picks)
        columns = lax.all_to_all(local, "lev", split_axis=3, concat_axis=2, tiled=True)
        vertical = jnp.einsum("vlk,mvkc->mvlc", vert, columns, preferred_element_type=jnp.float32)
        partial_value = jnp.sum(vertical * perturb.astype(jnp.float32), axis=0)
        static_portion = jnp.einsum(
            "tbu,tuo->tbo",
            static_vertical_root,
            static_control_vector,
            preferred_element_type=jnp.float32,
        )
        ens = lax.psum_scatter(partial_value, "mem", scatter_dimension=1, tiled=True)
        own_static = lax.dynamic_slice_in_dim(static_portion, first_level, level_rows, 1)
        increment = ens_gain * ens + STATIC_WEIGHT * own_static
        grad_block = observe(increment, obs_index, obs_value, precision_obs)
        gradient_field_total = lax.all_gather(grad_block, "mem", axis=1, tiled=True)
        static_gradient = static_control_vector.astype(jnp.float32) + STATIC_WEIGHT * jnp.einsum(
            "otn,ote->one", static_forward, gradient_field_total, precision=lax.Precision.HIGHEST
        )
        weighted_innovations = (ens_gain * gradient_field_total)[None] * perturb.astype(jnp.float32)
        backward_field = jnp.einsum(
            "vkl,mvkc->mvlc",
            vertical_forward,
            weighted_innovations,
            precision=lax.Precision.HIGHEST,
        ).astype(jnp.bfloat16)
        levels = lax.all_to_all(backward_field, "lev", split_axis=2, concat_axis=3, tiled=True)
        adjoint = horizontal_adjoint(levels, tiles, picks)
        current = control.astype(jnp.float32)
        control = (current - TAU * (current + adjoint)).astype(jnp.bfloat16)
        static_control_vector = (
            static_control_vector.astype(jnp.float32) - TAU * static_gradient
        ).astype(jnp.bfloat16)
    return (control, static_control_vector)


def split(value):
    high = value.astype(jnp.bfloat16)
    return high, (value - high.astype(jnp.float32)).astype(jnp.bfloat16)


def descent_kernel(
    ens_gain,
    control_hbm,
    static_hbm,
    perturb_hbm,
    tiles_hbm,
    offset_ref,
    vert_hbm,
    root_hbm,
    index_hbm,
    value_hbm,
    sigma_hbm,
    mask_hbm,
    control_out,
    static_out,
    perturb_ref,
    tiles_ref,
    vert_ref,
    root_ref,
    index_ref,
    value_ref,
    sigma_ref,
    mask_ref,
    dense,
    state,
    static_state,
    rows_in,
    inc0,
    precision_obs,
    hot_row,
    hot_col,
    fwd_send,
    fwd_recv,
    sum_send,
    sum_recv,
    grad_recv,
    bwd_send,
    bwd_recv,
    send_sem,
    recv_sem,
    fetch_sem,
):
    members, variables, per_lev, columns = control_hbm.shape
    n_lev = lax.axis_size("lev")
    n_mem = lax.axis_size("mem")
    levels = vert_ref.shape[1]
    per_mem = levels // n_mem
    width = static_state.shape[2]
    block = tiles_ref.shape[1]
    slots = tiles_ref.shape[0]
    count = columns // block
    chunk = members * per_lev
    my_lev = lax.axis_index("lev")
    my_mem = lax.axis_index("mem")

    barrier = pltpu.get_barrier_semaphore()
    for step in range(1, n_lev):
        pl.semaphore_signal(
            barrier, inc=1, device_id={"lev": lax.rem(my_lev + step, n_lev)}, device_id_type=MESH
        )
    for step in range(1, n_mem):
        pl.semaphore_signal(
            barrier, inc=1, device_id={"mem": lax.rem(my_mem + step, n_mem)}, device_id_type=MESH
        )

    tiles_copy = pltpu.make_async_copy(tiles_hbm, tiles_ref, fetch_sem.at[0])
    tiles_copy.start()
    for v in range(variables):
        for m in range(members):
            pltpu.make_async_copy(
                control_hbm.at[m, v],
                state.at[pl.ds(v * chunk + m * per_lev, per_lev)],
                fetch_sem.at[1],
            ).start()
    late = []
    for place, (source, target) in enumerate(
        (
            (root_hbm, root_ref),
            (static_hbm, static_state),
            (index_hbm, index_ref),
            (vert_hbm, vert_ref),
            (perturb_hbm, perturb_ref),
            (value_hbm, value_ref),
            (sigma_hbm, sigma_ref),
            (mask_hbm, mask_ref),
        )
    ):
        late.append(pltpu.make_async_copy(source, target, fetch_sem.at[2 + place]))
        late[-1].start()
    tiles_copy.wait()

    lane = lax.broadcasted_iota(jnp.int32, (1, width), 1)
    wide = []
    for slot in range(slots):
        tile = tiles_ref[slot].astype(jnp.float32)
        wide.append(jnp.concatenate([tile] * (width // block), axis=1))
    sources = []
    for group in range(columns // width):
        per_slot = []
        for slot in range(slots):
            vec = jnp.zeros((1, width), jnp.int32)
            for part in range(width // block):
                b = group * (width // block) + part
                src = lax.rem(lax.rem(b + offset_ref[slot, b], count) + count, count)
                vec = jnp.where(lane >= part * block, src, vec)
            per_slot.append(vec)
        sources.append(per_slot)

    def build(j, carry):
        for group in range(columns // width):
            total = jnp.zeros((block, width), jnp.float32)
            for slot in range(slots):
                total = total + jnp.where(sources[group][slot] == j, wide[slot], 0.0)
            dense[pl.ds(pl.multiple_of(j * block, block), block), group * width : (group + 1) * width] = (
                total.astype(jnp.bfloat16)
            )
        return carry

    lax.fori_loop(0, count, build, 0)
    pltpu.make_async_copy(state, state, fetch_sem.at[1]).wait()
    pl.semaphore_wait(barrier, n_lev - 1 + n_mem - 1)

    def lev_copy(send, recv, turn, phase, v, peer):
        return pltpu.make_async_remote_copy(
            src_ref=send.at[turn, v, peer],
            dst_ref=recv.at[turn, v, my_lev],
            send_sem=send_sem.at[turn, phase, v],
            recv_sem=recv_sem.at[turn, phase, v],
            device_id={"lev": peer},
            device_id_type=MESH,
        )

    def mem_copy(src, dst, turn, phase, v, peer):
        return pltpu.make_async_remote_copy(
            src_ref=src,
            dst_ref=dst,
            send_sem=send_sem.at[turn, phase, v],
            recv_sem=recv_sem.at[turn, phase, v],
            device_id={"mem": peer},
            device_id_type=MESH,
        )

    def await_blocks(buffer, sem, turn, phase, v, blocks):
        part = buffer.at[turn, v, pl.ds(0, blocks)]
        pltpu.make_async_copy(part, part, sem.at[turn, phase, v]).wait()

    half = 2 * width
    cut = (variables + 1) // 2
    groups = [g for g in (range(cut), range(cut, variables)) if len(g)]

    def forward(turn, group):
        rows = slice(group[0] * chunk, (group[-1] + 1) * chunk)
        for pair in range(columns // half):
            local = jnp.dot(
                state[rows, :],
                dense[:, pair * half : (pair + 1) * half],
                preferred_element_type=jnp.float32,
            ).astype(jnp.bfloat16)
            for place, v in enumerate(group):
                for side in range(2):
                    fwd_send[turn, v, pair * 2 + side] = local[
                        place * chunk : (place + 1) * chunk, side * width : (side + 1) * width
                    ]
        for v in group:
            for step in range(1, n_lev):
                lev_copy(fwd_send, fwd_recv, turn, 0, v, lax.rem(my_lev + step, n_lev)).start()
        for v in group:
            fwd_recv[turn, v, my_lev] = fwd_send[turn, v, my_lev]

    def static_forward():
        first = pl.multiple_of(my_mem * per_mem, per_mem)
        for v in range(variables):
            inc0[v * per_mem : (v + 1) * per_mem, :] = STATIC_WEIGHT * jnp.dot(
                root_ref[v, pl.ds(first, per_mem), :],
                static_state[v],
                preferred_element_type=jnp.float32,
            )

    def member_sum(turn, v):
        await_blocks(fwd_recv, recv_sem, turn, 0, v, n_lev - 1)
        cols = [
            fwd_recv[turn, v, :, m * per_lev : (m + 1) * per_lev, :].reshape(levels, width)
            for m in range(members)
        ]
        vertical = jnp.dot(
            vert_ref[v], jnp.concatenate(cols, axis=1), preferred_element_type=jnp.float32
        )
        total = None
        for m in range(members):
            term = vertical[:, m * width : (m + 1) * width] * perturb_ref[m, v].astype(jnp.float32)
            total = term if total is None else total + term
        sum_send[turn, v] = total.reshape(n_mem, per_mem, width)
        for step in range(1, n_mem):
            peer = lax.rem(my_mem + step, n_mem)
            mem_copy(
                sum_send.at[turn, v, peer], sum_recv.at[turn, v, my_mem], turn, 1, v, peer
            ).start()
        sum_recv[turn, v, my_mem] = sum_send[turn, v, my_mem]

    def observe_one(turn, v):
        await_blocks(sum_recv, recv_sem, turn, 1, v, n_mem - 1)
        own = slice(v * per_mem, (v + 1) * per_mem)
        increment = ens_gain * jnp.sum(sum_recv[turn, v], axis=0) + inc0[own, :]
        high, low = split(increment)
        picked = lax.dot_general(
            jnp.concatenate([high, low], axis=1),
            hot_row[own, :],
            (((0,), (0,)), ((), ())),
            preferred_element_type=jnp.float32,
        )
        seen = jnp.sum((picked[:width] + picked[width:]) * hot_col[...], axis=0, keepdims=True)
        resid = precision_obs[...] * (seen - value_ref[...])
        spread = lax.dot_general(
            hot_row[own, :],
            (hot_col[...] * resid).astype(jnp.bfloat16),
            (((1,), (1,)), ((), ())),
            preferred_element_type=jnp.float32,
        )
        grad_recv[turn, v, my_mem] = spread.astype(jnp.bfloat16)
        for step in range(1, n_mem):
            peer = lax.rem(my_mem + step, n_mem)
            mem_copy(
                grad_recv.at[turn, v, my_mem], grad_recv.at[turn, v, my_mem], turn, 2, v, peer
            ).start()

    def vertical_adjoint(turn, v):
        await_blocks(grad_recv, recv_sem, turn, 2, v, n_mem - 1)
        field = grad_recv[turn, v].reshape(levels, width).astype(jnp.float32)
        parts = [
            split((ens_gain * field) * perturb_ref[m, v].astype(jnp.float32)) for m in range(members)
        ]
        product = lax.dot_general(
            vert_ref[v],
            jnp.concatenate([p[0] for p in parts] + [p[1] for p in parts], axis=1),
            (((0,), (0,)), ((), ())),
            preferred_element_type=jnp.float32,
        )
        back = product[:, : members * width] + product[:, members * width :]
        for m in range(members):
            bwd_send[turn, v, :, m * per_lev : (m + 1) * per_lev, :] = (
                back[:, m * width : (m + 1) * width]
                .astype(jnp.bfloat16)
                .reshape(n_lev, per_lev, width)
            )
        for step in range(1, n_lev):
            lev_copy(bwd_send, bwd_recv, turn, 3, v, lax.rem(my_lev + step, n_lev)).start()
        bwd_recv[turn, v, my_lev] = bwd_send[turn, v, my_lev]

    def static_update(turn):
        for v in range(variables):
            product = lax.dot_general(
                root_ref[v],
                grad_recv[turn, v].reshape(levels, width),
                (((0,), (0,)), ((), ())),
                preferred_element_type=jnp.float32,
            )
            current = static_state[v].astype(jnp.float32)
            gradient = current + STATIC_WEIGHT * product
            static_state[v] = (current - TAU * gradient).astype(jnp.bfloat16)

    def horizontal_update(turn, group):
        rows = slice(group[0] * chunk, (group[-1] + 1) * chunk)
        for v in group:
            await_blocks(bwd_recv, recv_sem, turn, 3, v, n_lev - 1)
            for peer in range(n_lev):
                rows_in[v * chunk : (v + 1) * chunk, peer * width : (peer + 1) * width] = bwd_recv[
                    turn, v, peer
                ]
        for pair in range(columns // half):
            here = slice(pair * half, (pair + 1) * half)
            adjoint = lax.dot_general(
                rows_in[rows, :],
                dense[here, :],
                (((1,), (1,)), ((), ())),
                preferred_element_type=jnp.float32,
            )
            current = state[rows, here].astype(jnp.float32)
            state[rows, here] = (current - TAU * (current + adjoint)).astype(jnp.bfloat16)

    for group in groups:
        forward(0, group)
    for copy in late:
        copy.wait()
    static_forward()
    where_obs = index_ref[...]
    row_of = where_obs // width
    col_of = where_obs - row_of * width
    hot_row[...] = jnp.where(
        lax.broadcasted_iota(jnp.int32, hot_row.shape, 0) == row_of, 1.0, 0.0
    ).astype(jnp.bfloat16)
    hot_col[...] = jnp.where(lax.broadcasted_iota(jnp.int32, hot_col.shape, 0) == col_of, 1.0, 0.0)
    weights = jnp.where(mask_ref[...] == 1, jnp.float32(1.0), jnp.float32(HUBER_LOW))
    precision_obs[...] = weights / (sigma_ref[...] * sigma_ref[...])

    for turn in range(ITERS):
        for tick in range(variables + 4):
            if tick < variables:
                member_sum(turn, tick)
            if 0 <= tick - 2 < variables:
                observe_one(turn, tick - 2)
            if 0 <= tick - 4 < variables:
                vertical_adjoint(turn, tick - 4)
        static_update(turn)
        if turn + 1 < ITERS:
            static_forward()
        for group in groups:
            horizontal_update(turn, group)
            if turn + 1 < ITERS:
                forward(turn + 1, group)

    for v in range(variables):
        for m in range(members):
            control_out[m, v] = state[v * chunk + m * per_lev : v * chunk + (m + 1) * per_lev, :]
    static_out[...] = static_state[...]

    def drain(turn, carry):
        for v in range(variables):
            await_blocks(fwd_send, send_sem, turn, 0, v, n_lev - 1)
            await_blocks(sum_send, send_sem, turn, 1, v, n_mem - 1)
            await_blocks(grad_recv, send_sem, turn, 2, v, n_mem - 1)
            await_blocks(bwd_send, send_sem, turn, 3, v, n_lev - 1)
        return carry

    lax.fori_loop(0, ITERS, drain, 0)


def fused(
    control,
    static_control_vector,
    perturb,
    tiles,
    block_offset,
    vert,
    static_vertical_root,
    obs_index,
    obs_value,
    obs_sigma,
    huber_mask,
):
    members, variables, per_lev, columns = control.shape
    n_lev, n_mem = lax.axis_size("lev"), lax.axis_size("mem")
    levels, width = static_control_vector.shape[1:]
    per_mem = levels // n_mem
    chunk = members * per_lev
    observations = obs_index.shape[0]
    rows = variables * chunk
    ens_gain = ENS_W / math.sqrt(members * n_mem)
    vmem = pl.BlockSpec(memory_space=pltpu.VMEM)
    lev_buffer = pltpu.VMEM((ITERS, variables, n_lev, chunk, width), jnp.bfloat16)
    mem_buffer = pltpu.VMEM((ITERS, variables, n_mem, per_mem, width), jnp.float32)
    in_specs = [pl.BlockSpec(memory_space=pl.ANY)] * 11
    in_specs[4] = pl.BlockSpec(memory_space=pltpu.SMEM)
    flat = (1, observations)
    return pl.pallas_call(
        functools.partial(descent_kernel, ens_gain),
        out_shape=(
            jax.ShapeDtypeStruct(control.shape, control.dtype),
            jax.ShapeDtypeStruct(static_control_vector.shape, static_control_vector.dtype),
        ),
        in_specs=in_specs,
        out_specs=(vmem, vmem),
        scratch_shapes=[
            pltpu.VMEM(perturb.shape, perturb.dtype),
            pltpu.VMEM(tiles.shape, tiles.dtype),
            pltpu.VMEM(vert.shape, vert.dtype),
            pltpu.VMEM(static_vertical_root.shape, static_vertical_root.dtype),
            pltpu.VMEM(flat, obs_index.dtype),
            pltpu.VMEM(flat, obs_value.dtype),
            pltpu.VMEM(flat, obs_sigma.dtype),
            pltpu.VMEM(flat, huber_mask.dtype),
            pltpu.VMEM((columns, columns), jnp.bfloat16),
            pltpu.VMEM((rows, columns), jnp.bfloat16),
            pltpu.VMEM((variables, levels, width), jnp.bfloat16),
            pltpu.VMEM((rows, columns), jnp.bfloat16),
            pltpu.VMEM((variables * per_mem, width), jnp.float32),
            pltpu.VMEM(flat, jnp.float32),
            pltpu.VMEM((variables * per_mem, observations), jnp.bfloat16),
            pltpu.VMEM((width, observations), jnp.float32),
            lev_buffer,
            lev_buffer,
            mem_buffer,
            mem_buffer,
            pltpu.VMEM((ITERS, variables, n_mem, per_mem, width), jnp.bfloat16),
            lev_buffer,
            lev_buffer,
            pltpu.SemaphoreType.DMA((ITERS, 4, variables)),
            pltpu.SemaphoreType.DMA((ITERS, 4, variables)),
            pltpu.SemaphoreType.DMA((10,)),
        ],
        compiler_params=pltpu.CompilerParams(
            collective_id=0, has_side_effects=True, vmem_limit_bytes=60 * 1024 * 1024
        ),
    )(
        control,
        static_control_vector,
        perturb,
        tiles,
        block_offset.T,
        vert,
        static_vertical_root,
        obs_index.reshape(flat),
        obs_value.reshape(flat),
        obs_sigma.reshape(flat),
        huber_mask.reshape(flat),
    )


def suits(control, static_control_vector, tiles):
    per_lev, columns = control.shape[2:]
    levels, width = static_control_vector.shape[1:]
    return (
        per_lev % 16 == 0
        and width % 128 == 0
        and columns % (2 * width) == 0
        and width % tiles.shape[1] == 0
        and (levels // lax.axis_size("mem")) % 16 == 0
        and columns <= 2048
    )


def descent(*arguments):
    if suits(arguments[0], arguments[1], arguments[3]):
        return fused(*arguments)
    return on_device(*arguments)


def solution(mesh):
    placed = (
        P("mem", None, "lev", None),
        P(None, None, "lev"),
        P("mem", None, None, "lev"),
        P(),
        P(),
        P(),
        P(),
        P(("lev", "mem")),
        P(("lev", "mem")),
        P(("lev", "mem")),
        P(("lev", "mem")),
    )
    return jax.shard_map(
        descent,
        mesh=mesh,
        in_specs=placed,
        out_specs=(P("mem", None, "lev", None), P(None, None, "lev")),
        check_vma=False,
    )
```

```python
import functools
import math

import jax
import jax.numpy as jnp
from jax import lax
from jax.experimental import pallas as pl
from jax.experimental.pallas import tpu as pltpu
from jax.sharding import PartitionSpec as P

ITERS = 2


ENS_W = 0.85
STATIC_WEIGHT = 0.5
TAU = 0.5
HUBER_LOW = 0.3
MESH = pl.DeviceIdType.MESH


def selectors(block_offset):
    count = block_offset.shape[0]
    blocks = jnp.arange(count, dtype=jnp.int32)
    source = (blocks[:, None] + block_offset) % count
    return (source.T[:, :, None] == blocks[None, None, :]).astype(jnp.bfloat16)


def horizontal(field, tiles, picks):
    count = picks.shape[1]
    width = tiles.shape[1]
    shaped = field.reshape(field.shape[:-1] + (count, width))
    total = None
    for slot in range(tiles.shape[0]):
        moved = jnp.einsum(
            "bj,...jc->...bc", picks[slot], shaped, preferred_element_type=jnp.float32
        ).astype(jnp.bfloat16)
        term = jnp.einsum("...bc,cd->...bd", moved, tiles[slot], preferred_element_type=jnp.float32)
        total = term if total is None else total + term
    return total.reshape(field.shape).astype(jnp.bfloat16)


def horizontal_adjoint(field, tiles, picks):
    count = picks.shape[1]
    width = tiles.shape[1]
    shaped = field.reshape(field.shape[:-1] + (count, width))
    total = None
    for slot in range(tiles.shape[0]):
        term = jnp.einsum(
            "...bc,dc->...bd", shaped, tiles[slot], preferred_element_type=jnp.float32
        )
        moved = jnp.einsum(
            "bj,...bd->...jd",
            picks[slot].astype(jnp.float32),
            term,
            precision=lax.Precision.HIGHEST,
        )
        total = moved if total is None else total + moved
    return total.reshape(field.shape)


def observe(block, obs_index, obs_value, precision_obs):
    flat = block.reshape(-1)
    seen = flat[obs_index]
    resid = precision_obs * (seen - obs_value)
    return jnp.zeros_like(flat).at[obs_index].add(resid).reshape(block.shape)


def on_device(
    control,
    static_control_vector,
    perturb,
    tiles,
    block_offset,
    vert,
    static_vertical_root,
    obs_index,
    obs_value,
    obs_sigma,
    huber_mask,
):
    picks = selectors(block_offset)
    members_all = control.shape[0] * lax.axis_size("mem")
    ens_gain = ENS_W / math.sqrt(members_all)
    level_rows = static_control_vector.shape[1] // lax.axis_size("mem")
    first_level = lax.axis_index("mem") * level_rows
    weights = jnp.where(huber_mask == 1, jnp.float32(1.0), jnp.float32(HUBER_LOW))
    precision_obs = weights / (obs_sigma * obs_sigma)
    vertical_forward = vert.astype(jnp.float32)
    static_forward = static_vertical_root.astype(jnp.float32)
    for turn in range(ITERS):
        local = horizontal(control, tiles, picks)
        columns = lax.all_to_all(local, "lev", split_axis=3, concat_axis=2, tiled=True)
        vertical = jnp.einsum("vlk,mvkc->mvlc", vert, columns, preferred_element_type=jnp.float32)
        partial_value = jnp.sum(vertical * perturb.astype(jnp.float32), axis=0)
        static_portion = jnp.einsum(
            "tbu,tuo->tbo",
            static_vertical_root,
            static_control_vector,
            preferred_element_type=jnp.float32,
        )
        ens = lax.psum_scatter(partial_value, "mem", scatter_dimension=1, tiled=True)
        own_static = lax.dynamic_slice_in_dim(static_portion, first_level, level_rows, 1)
        increment = ens_gain * ens + STATIC_WEIGHT * own_static
        grad_block = observe(increment, obs_index, obs_value, precision_obs)
        gradient_field_total = lax.all_gather(grad_block, "mem", axis=1, tiled=True)
        static_gradient = static_control_vector.astype(jnp.float32) + STATIC_WEIGHT * jnp.einsum(
            "otn,ote->one", static_forward, gradient_field_total, precision=lax.Precision.HIGHEST
        )
        weighted_innovations = (ens_gain * gradient_field_total)[None] * perturb.astype(jnp.float32)
        backward_field = jnp.einsum(
            "vkl,mvkc->mvlc",
            vertical_forward,
            weighted_innovations,
            precision=lax.Precision.HIGHEST,
        ).astype(jnp.bfloat16)
        levels = lax.all_to_all(backward_field, "lev", split_axis=2, concat_axis=3, tiled=True)
        adjoint = horizontal_adjoint(levels, tiles, picks)
        current = control.astype(jnp.float32)
        control = (current - TAU * (current + adjoint)).astype(jnp.bfloat16)
        static_control_vector = (
            static_control_vector.astype(jnp.float32) - TAU * static_gradient
        ).astype(jnp.bfloat16)
    return (control, static_control_vector)


def split(value):
    high = value.astype(jnp.bfloat16)
    return high, (value - high.astype(jnp.float32)).astype(jnp.bfloat16)


def descent_kernel(
    ens_gain,
    control_hbm,
    static_hbm,
    perturb_hbm,
    tiles_hbm,
    offset_ref,
    vert_hbm,
    root_hbm,
    index_hbm,
    value_hbm,
    sigma_hbm,
    mask_hbm,
    control_out,
    static_out,
    perturb_ref,
    tiles_ref,
    vert_ref,
    root_ref,
    index_ref,
    value_ref,
    sigma_ref,
    mask_ref,
    dense,
    state,
    static_state,
    rows_in,
    inc0,
    precision_obs,
    hot_row,
    hot_col,
    fwd_send,
    fwd_recv,
    sum_send,
    sum_recv,
    grad_recv,
    bwd_send,
    bwd_recv,
    send_sem,
    recv_sem,
    fetch_sem,
):
    members, variables, per_lev, columns = control_hbm.shape
    n_lev = lax.axis_size("lev")
    n_mem = lax.axis_size("mem")
    levels = vert_ref.shape[1]
    per_mem = levels // n_mem
    width = static_state.shape[2]
    block = tiles_ref.shape[1]
    slots = tiles_ref.shape[0]
    count = columns // block
    chunk = members * per_lev
    my_lev = lax.axis_index("lev")
    my_mem = lax.axis_index("mem")

    barrier = pltpu.get_barrier_semaphore()
    for step in range(1, n_lev):
        pl.semaphore_signal(
            barrier, inc=1, device_id={"lev": lax.rem(my_lev + step, n_lev)}, device_id_type=MESH
        )
    for step in range(1, n_mem):
        pl.semaphore_signal(
            barrier, inc=1, device_id={"mem": lax.rem(my_mem + step, n_mem)}, device_id_type=MESH
        )

    tiles_copy = pltpu.make_async_copy(tiles_hbm, tiles_ref, fetch_sem.at[0])
    tiles_copy.start()
    for v in range(variables):
        for m in range(members):
            pltpu.make_async_copy(
                control_hbm.at[m, v],
                state.at[pl.ds(v * chunk + m * per_lev, per_lev)],
                fetch_sem.at[1],
            ).start()
    late = []
    for place, (source, target) in enumerate(
        (
            (root_hbm, root_ref),
            (static_hbm, static_state),
            (index_hbm, index_ref),
            (vert_hbm, vert_ref),
            (perturb_hbm, perturb_ref),
            (value_hbm, value_ref),
            (sigma_hbm, sigma_ref),
            (mask_hbm, mask_ref),
        )
    ):
        late.append(pltpu.make_async_copy(source, target, fetch_sem.at[2 + place]))
        late[-1].start()
    tiles_copy.wait()

    lane = lax.broadcasted_iota(jnp.int32, (1, width), 1)
    wide = []
    for slot in range(slots):
        tile = tiles_ref[slot].astype(jnp.float32)
        wide.append(jnp.concatenate([tile] * (width // block), axis=1))
    sources = []
    for group in range(columns // width):
        per_slot = []
        for slot in range(slots):
            vec = jnp.zeros((1, width), jnp.int32)
            for part in range(width // block):
                b = group * (width // block) + part
                src = lax.rem(lax.rem(b + offset_ref[slot, b], count) + count, count)
                vec = jnp.where(lane >= part * block, src, vec)
            per_slot.append(vec)
        sources.append(per_slot)

    def build(j, carry):
        for group in range(columns // width):
            total = jnp.zeros((block, width), jnp.float32)
            for slot in range(slots):
                total = total + jnp.where(sources[group][slot] == j, wide[slot], 0.0)
            dense[pl.ds(pl.multiple_of(j * block, block), block), group * width : (group + 1) * width] = (
                total.astype(jnp.bfloat16)
            )
        return carry

    lax.fori_loop(0, count, build, 0)
    pltpu.make_async_copy(state, state, fetch_sem.at[1]).wait()
    pl.semaphore_wait(barrier, n_lev - 1 + n_mem - 1)

    def lev_copy(send, recv, turn, phase, v, peer):
        return pltpu.make_async_remote_copy(
            src_ref=send.at[turn, v, peer],
            dst_ref=recv.at[turn, v, my_lev],
            send_sem=send_sem.at[turn, phase, v],
            recv_sem=recv_sem.at[turn, phase, v],
            device_id={"lev": peer},
            device_id_type=MESH,
        )

    def mem_copy(src, dst, turn, phase, v, peer):
        return pltpu.make_async_remote_copy(
            src_ref=src,
            dst_ref=dst,
            send_sem=send_sem.at[turn, phase, v],
            recv_sem=recv_sem.at[turn, phase, v],
            device_id={"mem": peer},
            device_id_type=MESH,
        )

    def await_blocks(buffer, sem, turn, phase, v, blocks):
        part = buffer.at[turn, v, pl.ds(0, blocks)]
        pltpu.make_async_copy(part, part, sem.at[turn, phase, v]).wait()

    half = 2 * width
    cut = (variables + 1) // 2
    groups = [g for g in (range(cut), range(cut, variables)) if len(g)]

    def forward(turn, group):
        rows = slice(group[0] * chunk, (group[-1] + 1) * chunk)
        for pair in range(columns // half):
            local = jnp.dot(
                state[rows, :],
                dense[:, pair * half : (pair + 1) * half],
                preferred_element_type=jnp.float32,
            ).astype(jnp.bfloat16)
            for place, v in enumerate(group):
                for side in range(2):
                    fwd_send[turn, v, pair * 2 + side] = local[
                        place * chunk : (place + 1) * chunk, side * width : (side + 1) * width
                    ]
        for v in group:
            for step in range(1, n_lev):
                lev_copy(fwd_send, fwd_recv, turn, 0, v, lax.rem(my_lev + step, n_lev)).start()
        for v in group:
            fwd_recv[turn, v, my_lev] = fwd_send[turn, v, my_lev]

    def static_forward():
        first = pl.multiple_of(my_mem * per_mem, per_mem)
        for v in range(variables):
            inc0[v * per_mem : (v + 1) * per_mem, :] = STATIC_WEIGHT * jnp.dot(
                root_ref[v, pl.ds(first, per_mem), :],
                static_state[v],
                preferred_element_type=jnp.float32,
            )

    def member_sum(turn, v):
        await_blocks(fwd_recv, recv_sem, turn, 0, v, n_lev - 1)
        cols = [
            fwd_recv[turn, v, :, m * per_lev : (m + 1) * per_lev, :].reshape(levels, width)
            for m in range(members)
        ]
        vertical = jnp.dot(
            vert_ref[v], jnp.concatenate(cols, axis=1), preferred_element_type=jnp.float32
        )
        total = None
        for m in range(members):
            term = vertical[:, m * width : (m + 1) * width] * perturb_ref[m, v].astype(jnp.float32)
            total = term if total is None else total + term
        sum_send[turn, v] = total.reshape(n_mem, per_mem, width)
        for step in range(1, n_mem):
            peer = lax.rem(my_mem + step, n_mem)
            mem_copy(
                sum_send.at[turn, v, peer], sum_recv.at[turn, v, my_mem], turn, 1, v, peer
            ).start()
        sum_recv[turn, v, my_mem] = sum_send[turn, v, my_mem]

    def observe_one(turn, v):
        await_blocks(sum_recv, recv_sem, turn, 1, v, n_mem - 1)
        own = slice(v * per_mem, (v + 1) * per_mem)
        increment = ens_gain * jnp.sum(sum_recv[turn, v], axis=0) + inc0[own, :]
        high, low = split(increment)
        picked = lax.dot_general(
            jnp.concatenate([high, low], axis=1),
            hot_row[own, :],
            (((0,), (0,)), ((), ())),
            preferred_element_type=jnp.float32,
        )
        seen = jnp.sum((picked[:width] + picked[width:]) * hot_col[...], axis=0, keepdims=True)
        resid = precision_obs[...] * (seen - value_ref[...])
        spread = lax.dot_general(
            hot_row[own, :],
            (hot_col[...] * resid).astype(jnp.bfloat16),
            (((1,), (1,)), ((), ())),
            preferred_element_type=jnp.float32,
        )
        grad_recv[turn, v, my_mem] = spread.astype(jnp.bfloat16)
        for step in range(1, n_mem):
            peer = lax.rem(my_mem + step, n_mem)
            mem_copy(
                grad_recv.at[turn, v, my_mem], grad_recv.at[turn, v, my_mem], turn, 2, v, peer
            ).start()

    def vertical_adjoint(turn, v):
        await_blocks(grad_recv, recv_sem, turn, 2, v, n_mem - 1)
        field = grad_recv[turn, v].reshape(levels, width).astype(jnp.float32)
        parts = [
            split((ens_gain * field) * perturb_ref[m, v].astype(jnp.float32)) for m in range(members)
        ]
        product = lax.dot_general(
            vert_ref[v],
            jnp.concatenate([p[0] for p in parts] + [p[1] for p in parts], axis=1),
            (((0,), (0,)), ((), ())),
            preferred_element_type=jnp.float32,
        )
        back = product[:, : members * width] + product[:, members * width :]
        for m in range(members):
            bwd_send[turn, v, :, m * per_lev : (m + 1) * per_lev, :] = (
                back[:, m * width : (m + 1) * width]
                .astype(jnp.bfloat16)
                .reshape(n_lev, per_lev, width)
            )
        for step in range(1, n_lev):
            lev_copy(bwd_send, bwd_recv, turn, 3, v, lax.rem(my_lev + step, n_lev)).start()
        bwd_recv[turn, v, my_lev] = bwd_send[turn, v, my_lev]

    def static_update(turn):
        for v in range(variables):
            product = lax.dot_general(
                root_ref[v],
                grad_recv[turn, v].reshape(levels, width),
                (((0,), (0,)), ((), ())),
                preferred_element_type=jnp.float32,
            )
            current = static_state[v].astype(jnp.float32)
            gradient = current + STATIC_WEIGHT * product
            static_state[v] = (current - TAU * gradient).astype(jnp.bfloat16)

    def horizontal_update(turn, group):
        rows = slice(group[0] * chunk, (group[-1] + 1) * chunk)
        for v in group:
            await_blocks(bwd_recv, recv_sem, turn, 3, v, n_lev - 1)
            for peer in range(n_lev):
                rows_in[v * chunk : (v + 1) * chunk, peer * width : (peer + 1) * width] = bwd_recv[
                    turn, v, peer
                ]
        for pair in range(columns // half):
            here = slice(pair * half, (pair + 1) * half)
            adjoint = lax.dot_general(
                rows_in[rows, :],
                dense[here, :],
                (((1,), (1,)), ((), ())),
                preferred_element_type=jnp.float32,
            )
            current = state[rows, here].astype(jnp.float32)
            state[rows, here] = (current - TAU * (current + adjoint)).astype(jnp.bfloat16)

    for group in groups:
        forward(0, group)
    for copy in late:
        copy.wait()
    static_forward()
    where_obs = index_ref[...]
    row_of = where_obs // width
    col_of = where_obs - row_of * width
    hot_row[...] = jnp.where(
        lax.broadcasted_iota(jnp.int32, hot_row.shape, 0) == row_of, 1.0, 0.0
    ).astype(jnp.bfloat16)
    hot_col[...] = jnp.where(lax.broadcasted_iota(jnp.int32, hot_col.shape, 0) == col_of, 1.0, 0.0)
    weights = jnp.where(mask_ref[...] == 1, jnp.float32(1.0), jnp.float32(HUBER_LOW))
    precision_obs[...] = weights / (sigma_ref[...] * sigma_ref[...])

    for turn in range(ITERS):
        for tick in range(variables + 3):
            if tick < variables:
                member_sum(turn, tick)
            if 0 <= tick - 1 < variables:
                observe_one(turn, tick - 1)
            if 0 <= tick - 3 < variables:
                vertical_adjoint(turn, tick - 3)
        static_update(turn)
        if turn + 1 < ITERS:
            static_forward()
        for group in groups:
            horizontal_update(turn, group)
            if turn + 1 < ITERS:
                forward(turn + 1, group)

    for v in range(variables):
        for m in range(members):
            control_out[m, v] = state[v * chunk + m * per_lev : v * chunk + (m + 1) * per_lev, :]
    static_out[...] = static_state[...]

    def drain(turn, carry):
        for v in range(variables):
            await_blocks(fwd_send, send_sem, turn, 0, v, n_lev - 1)
            await_blocks(sum_send, send_sem, turn, 1, v, n_mem - 1)
            await_blocks(grad_recv, send_sem, turn, 2, v, n_mem - 1)
            await_blocks(bwd_send, send_sem, turn, 3, v, n_lev - 1)
        return carry

    lax.fori_loop(0, ITERS, drain, 0)


def fused(
    control,
    static_control_vector,
    perturb,
    tiles,
    block_offset,
    vert,
    static_vertical_root,
    obs_index,
    obs_value,
    obs_sigma,
    huber_mask,
):
    members, variables, per_lev, columns = control.shape
    n_lev, n_mem = lax.axis_size("lev"), lax.axis_size("mem")
    levels, width = static_control_vector.shape[1:]
    per_mem = levels // n_mem
    chunk = members * per_lev
    observations = obs_index.shape[0]
    rows = variables * chunk
    ens_gain = ENS_W / math.sqrt(members * n_mem)
    vmem = pl.BlockSpec(memory_space=pltpu.VMEM)
    lev_buffer = pltpu.VMEM((ITERS, variables, n_lev, chunk, width), jnp.bfloat16)
    mem_buffer = pltpu.VMEM((ITERS, variables, n_mem, per_mem, width), jnp.float32)
    in_specs = [pl.BlockSpec(memory_space=pl.ANY)] * 11
    in_specs[4] = pl.BlockSpec(memory_space=pltpu.SMEM)
    flat = (1, observations)
    return pl.pallas_call(
        functools.partial(descent_kernel, ens_gain),
        out_shape=(
            jax.ShapeDtypeStruct(control.shape, control.dtype),
            jax.ShapeDtypeStruct(static_control_vector.shape, static_control_vector.dtype),
        ),
        in_specs=in_specs,
        out_specs=(vmem, vmem),
        scratch_shapes=[
            pltpu.VMEM(perturb.shape, perturb.dtype),
            pltpu.VMEM(tiles.shape, tiles.dtype),
            pltpu.VMEM(vert.shape, vert.dtype),
            pltpu.VMEM(static_vertical_root.shape, static_vertical_root.dtype),
            pltpu.VMEM(flat, obs_index.dtype),
            pltpu.VMEM(flat, obs_value.dtype),
            pltpu.VMEM(flat, obs_sigma.dtype),
            pltpu.VMEM(flat, huber_mask.dtype),
            pltpu.VMEM((columns, columns), jnp.bfloat16),
            pltpu.VMEM((rows, columns), jnp.bfloat16),
            pltpu.VMEM((variables, levels, width), jnp.bfloat16),
            pltpu.VMEM((rows, columns), jnp.bfloat16),
            pltpu.VMEM((variables * per_mem, width), jnp.float32),
            pltpu.VMEM(flat, jnp.float32),
            pltpu.VMEM((variables * per_mem, observations), jnp.bfloat16),
            pltpu.VMEM((width, observations), jnp.float32),
            lev_buffer,
            lev_buffer,
            mem_buffer,
            mem_buffer,
            pltpu.VMEM((ITERS, variables, n_mem, per_mem, width), jnp.bfloat16),
            lev_buffer,
            lev_buffer,
            pltpu.SemaphoreType.DMA((ITERS, 4, variables)),
            pltpu.SemaphoreType.DMA((ITERS, 4, variables)),
            pltpu.SemaphoreType.DMA((10,)),
        ],
        compiler_params=pltpu.CompilerParams(
            collective_id=0, has_side_effects=True, vmem_limit_bytes=60 * 1024 * 1024
        ),
    )(
        control,
        static_control_vector,
        perturb,
        tiles,
        block_offset.T,
        vert,
        static_vertical_root,
        obs_index.reshape(flat),
        obs_value.reshape(flat),
        obs_sigma.reshape(flat),
        huber_mask.reshape(flat),
    )


def suits(control, static_control_vector, tiles):
    per_lev, columns = control.shape[2:]
    levels, width = static_control_vector.shape[1:]
    return (
        per_lev % 16 == 0
        and width % 128 == 0
        and columns % (2 * width) == 0
        and width % tiles.shape[1] == 0
        and (levels // lax.axis_size("mem")) % 16 == 0
        and columns <= 2048
    )


def descent(*arguments):
    if suits(arguments[0], arguments[1], arguments[3]):
        return fused(*arguments)
    return on_device(*arguments)


def solution(mesh):
    placed = (
        P("mem", None, "lev", None),
        P(None, None, "lev"),
        P("mem", None, None, "lev"),
        P(),
        P(),
        P(),
        P(),
        P(("lev", "mem")),
        P(("lev", "mem")),
        P(("lev", "mem")),
        P(("lev", "mem")),
    )
    return jax.shard_map(
        descent,
        mesh=mesh,
        in_specs=placed,
        out_specs=(P("mem", None, "lev", None), P(None, None, "lev")),
        check_vma=False,
    )
```
